32 devices in a mesh: groups: 2 (over y), seq: 16 (over z, x, core).
Axes of the slice: x: 2, y: 2, z: 4, core: 2. Of those that a mesh axis runs over, the one named last changes fastest.
Arguments:
- queries: bfloat16 [8192, 2048], P(('groups', 'seq')), parts along dimension 0, may hold values from -6 to 6
- key_inputs: bfloat16 [8192, 2048], P(('groups', 'seq')), parts along dimension 0, may hold values from -6 to 6
- values: bfloat16 [8192, 2048], P(('groups', 'seq')), parts along dimension 0, may hold values from -6 to 6
- short_taps: float32 [3, 3, 2048], replicated, may hold values from -3.6 to 3.6
- decay_rates: float32 [2, 2048], replicated, may hold values from 2.4414063e-05 to 0.05, as said below
- residues: float32 [2, 2048], replicated, may hold values from -6 to 6
- skip_gain: float32 [2048], replicated, may hold values from -6 to 6
- out_weight: bfloat16 [2048, 4096], P('seq'), may hold values from -0.125 to 0.125
- cotangent: bfloat16 [8192, 4096], P(('groups', 'seq')), parts along dimension 0, may hold values from -6 to 6
- doc_blocks: int32 [8], P('groups'), parts along dimension 0, may hold values from 1 to 16, 32 in all
Outputs:
- mixed_out: bfloat16 [8192, 4096], P(('groups', 'seq')), parts along dimension 0
- grad_queries: bfloat16 [8192, 2048], P(('groups', 'seq')), parts along dimension 0
- grad_keys: bfloat16 [8192, 2048], P(('groups', 'seq')), parts along dimension 0
- grad_values: bfloat16 [8192, 2048], P(('groups', 'seq')), parts along dimension 0
The draws below stay inside these ranges and needn't reach their ends.
There are 2 independent parts, one for each index of `groups`. The reference program is written for one: setup_inputs(seed, part) draws one part's arguments, and reference() takes and returns one part's arrays. A program takes and returns all parts, laid end to end along the dimension named above; an argument that names none is the same for every part. Nothing has to cross between parts.
Inputs may be any that keep to these rules, and one draw needn't show every extreme that they name: `doc_blocks`: documents fill the batch in order: the entries sum to 32, and the longest is exactly 16 blocks. `decay_rates`: positive decay rates.
All inputs are finite; a program needn't handle non-finite values.
Results may differ from the reference program's by a relative error of at most 0.0051.
Values may be sent and summed in bfloat16 or wider, within the bound.
A program may use at most 128 MiB of HBM per device.

```python
import math
import jax
import jax.numpy as jnp
import numpy as np
from jax import lax

D = 4096
TAPS = 3
CHAN = 2048
MODES = 2
BLOCK = 128
TOK_DEV = 256
TOKENS = 4096
NBLOCKS = 32
DOCS = 4
MOST = 16


def draw_decay_rates(key, part):
    pick_key, slow_key, fast_key = jax.random.split(key, 3)
    slow_share = 0.5
    reach = 8.0 * TOK_DEV
    chooser = jax.random.uniform(pick_key, (MODES, CHAN), jnp.float32)
    slow_rate = jnp.exp(jax.random.uniform(slow_key, (MODES, CHAN), jnp.float32, math.log(0.05 / reach), math.log(2.0 / reach)))
    fast_rate = jnp.exp(jax.random.uniform(fast_key, (MODES, CHAN), jnp.float32, math.log(0.005), math.log(0.05)))
    return jnp.where(chooser < slow_share, slow_rate, fast_rate).astype(jnp.float32)


def level_of(key, dims, cuts, least, high):
    loudness = 1.0
    for position, parts in cuts:
        heights = jax.random.uniform(jax.random.fold_in(jax.random.fold_in(key, 6), position), (parts,), jnp.float32, least / len(cuts), high / len(cuts))
        loudness = loudness * jnp.repeat(jnp.exp(heights), dims[position] // parts).reshape((-1,) + (1,) * (len(dims) - 1 - position))
    return loudness


def split_up(number_of, total, most, slope):
    loads = [(1 << 20) // math.isqrt(grade ** slope) + 1 for grade in range(2, number_of + 1)]
    rest, holding = total - most - (number_of - 1), [1] * (number_of - 1)
    while rest > 0:
        candidates = [i for i in range(number_of - 1) if holding[i] < most]
        whole, budget = sum([loads[i] for i in candidates]), rest
        for i in candidates:
            addition = min(most - holding[i], max(1, budget * loads[i] // whole), rest)
            holding[i] = holding[i] + addition
            rest = rest - addition
    return np.array([most] + holding)


def ragged_sizes(own_key, number_of, total, limit, lean):
    if number_of == 2:
        one = jax.random.randint(own_key, (), max(1, total - limit), min(limit, total - 1) + 1)
        return jnp.stack([one, total - one])
    lengths = jnp.asarray(split_up(number_of, total, limit, lean), jnp.int32)
    pairs = (number_of - 1) // 2
    donor, sink = lengths[1:1 + 2 * pairs:2], lengths[2:2 + 2 * pairs:2]
    margin = jnp.minimum(donor - 1, limit - sink)
    passed = jax.random.randint(jax.random.fold_in(own_key, 1), (pairs,), 0, 1 << 20) % (margin + 1)
    lengths = lengths.at[1:1 + 2 * pairs:2].set(donor - passed).at[2:2 + 2 * pairs:2].set(sink + passed)
    return lengths[jax.random.permutation(jax.random.fold_in(own_key, 2), number_of)]


def noise(stream_key, shape, spread, bound, shards=(), kind=jnp.bfloat16):
    drawn = spread * jax.random.normal(stream_key, shape, jnp.float32)
    if shards:
        drawn = drawn * level_of(stream_key, shape, shards, -0.22, 0.18)
    return jnp.clip(drawn, -bound, bound).astype(kind)


def setup_inputs(seed: int = 0, part: int = 0) -> dict:
    seeds = jax.random.split(jax.random.key(seed), 11)
    own_keys = jax.random.split(jax.random.fold_in(seeds[10], part), 11)
    queries = noise(own_keys[0], (TOKENS, CHAN), 1.0, 6.0, ((0, 16),))
    key_inputs = noise(own_keys[1], (TOKENS, CHAN), 1.0, 6.0, ((0, 16),))
    values = noise(own_keys[2], (TOKENS, CHAN), 1.0, 6.0, ((0, 16),))
    short_taps = noise(seeds[3], (3, TAPS, CHAN), 0.6, 3.6, (), jnp.float32)
    decay_rates = draw_decay_rates(jax.random.fold_in(seeds[10], 71), part)
    residues = noise(seeds[5], (MODES, CHAN), 1.0, 6.0, (), jnp.float32)
    skip_gain = noise(seeds[6], (CHAN,), 1.0, 6.0, (), jnp.float32)
    out_weight = noise(seeds[7], (CHAN, D), CHAN ** -0.5, 0.125, ((0, 16),))
    cotangent = noise(own_keys[8], (TOKENS, D), 1.0, 6.0, ((0, 16),))
    doc_blocks = ragged_sizes(own_keys[9], DOCS, NBLOCKS, MOST, 2).astype(jnp.int32)
    return {"queries": queries, "key_inputs": key_inputs, "values": values, "short_taps": short_taps, "decay_rates": decay_rates, "residues": residues, "skip_gain": skip_gain, "out_weight": out_weight, "cotangent": cotangent, "doc_blocks": doc_blocks}


def start_marks(doc_blocks):
    doc_ends = jnp.cumsum(doc_blocks)
    starts = doc_ends - doc_blocks
    block_index = jnp.arange(NBLOCKS, dtype=jnp.int32)
    marks = jnp.any(block_index[:, None] == starts[None, :], axis=1).astype(jnp.float32)
    head_mask = (jnp.arange(BLOCK) == 0).astype(jnp.float32)
    return (marks[:, None] * head_mask[None, :]).reshape(TOKENS)

def short_forward(inputs, tap_row, begins):
    inputs = inputs.astype(jnp.float32)
    lag_one = jnp.concatenate([jnp.zeros((1, CHAN), jnp.float32), inputs[:-1]], axis=0)
    lag_two = jnp.concatenate([jnp.zeros((2, CHAN), jnp.float32), inputs[:-2]], axis=0)
    prior_start = jnp.concatenate([jnp.zeros((1,), jnp.float32), begins[:-1]])
    keep_one = (1.0 - begins)[:, None]
    keep_two = keep_one * (1.0 - prior_start)[:, None]
    return tap_row[0] * inputs + tap_row[1] * keep_one * lag_one + tap_row[2] * keep_two * lag_two

def short_backward(gradient, tap_row, begins):
    lead_one = jnp.concatenate([gradient[1:], jnp.zeros((1, CHAN), jnp.float32)], axis=0)
    lead_two = jnp.concatenate([gradient[2:], jnp.zeros((2, CHAN), jnp.float32)], axis=0)
    next_one = jnp.concatenate([begins[1:], jnp.ones((1,), jnp.float32)])
    next_two = jnp.concatenate([begins[2:], jnp.ones((2,), jnp.float32)])
    keep_one = (1.0 - next_one)[:, None]
    keep_two = keep_one * (1.0 - next_two)[:, None]
    summed = tap_row[0] * gradient + tap_row[1] * keep_one * lead_one + tap_row[2] * keep_two * lead_two
    return summed.astype(jnp.bfloat16)

def decayed(inputs, decay_rates, filter_weight, resets, backward):
    factor = jnp.exp(-decay_rates)

    def advance(state, item):
        row_now, reset_now = item
        state = state * factor * (1.0 - reset_now) + row_now[None, :]
        return (state, lax.optimization_barrier(jnp.sum(state * filter_weight, axis=0)))
    initial = jnp.zeros((MODES, CHAN), jnp.float32)
    _, outputs = lax.scan(advance, initial, (inputs, resets), reverse=backward)
    return outputs

def reference(queries, key_inputs, values, short_taps, decay_rates, residues, skip_gain, out_weight, cotangent, doc_blocks):
    begins = start_marks(doc_blocks)
    q_short = short_forward(queries, short_taps[0], begins)
    k_short = short_forward(key_inputs, short_taps[1], begins)
    v_short = short_forward(values, short_taps[2], begins)
    product = k_short * v_short
    filter_weight = residues * jnp.sqrt(2.0 * decay_rates)
    conv_out = decayed(product, decay_rates, filter_weight, begins, False) + skip_gain * product
    gated = (q_short * conv_out).astype(jnp.bfloat16)
    mixed_out = jnp.dot(gated, out_weight, preferred_element_type=jnp.float32).astype(jnp.bfloat16)
    grad_gated = jnp.dot(cotangent, out_weight.T, preferred_element_type=jnp.float32)
    grad_qs = grad_gated * conv_out
    grad_conv = grad_gated * q_short
    doc_last = jnp.concatenate([begins[1:], jnp.ones((1,), jnp.float32)])
    grad_product = decayed(grad_conv, decay_rates, filter_weight, doc_last, True) + skip_gain * grad_conv
    grad_ks = grad_product * v_short
    grad_vs = grad_product * k_short
    return (mixed_out, short_backward(grad_qs, short_taps[0], begins), short_backward(grad_ks, short_taps[1], begins), short_backward(grad_vs, short_taps[2], begins))
```

```python
import functools

import jax
import jax.numpy as jnp
from jax import lax
from jax.experimental import pallas as pl
from jax.experimental.pallas import tpu as pltpu
from jax.sharding import PartitionSpec as P

BLOCK = 128
REACH = 8
Z_SIZE = 4
MESH_ID = pl.DeviceIdType.MESH
ROUTES = (("zxy", 7), ("zyx", 6), ("xyz", 3))
F32 = jnp.float32
BF16 = jnp.bfloat16


def last_axis(order, dz, dx, dy):
    moved = {"z": dz != 0, "x": dx != 0, "y": dy != 0}
    if dz == 0 and dx == 0:
        return -1 if dy == 0 else order.index("y")
    return max(i for i in range(3) if moved[order[i]])


def sends_of(order, dz, dx, dy):
    last = last_axis(order, dz, dx, dy)
    moves = []
    for i in range(3):
        axis = order[i]
        if i < last or (i == last and axis != "z"):
            continue
        if axis == "z":
            if dz >= 0:
                moves.append("up")
            if dz <= 0:
                moves.append("down")
        elif axis == "x":
            moves.append("x")
        elif not (dz == 0 and dx == 0):
            moves.append("y")
    return moves


def all_sites():
    sites = []
    for dz in range(-(Z_SIZE - 1), Z_SIZE):
        for dx in range(2):
            for dy in range(2):
                for r in range(len(ROUTES)):
                    sites.append((abs(dz) + dx + dy, dz, dx, dy, r))
    return sorted(sites)


def send_slots():
    slots = {}
    for _, dz, dx, dy, r in all_sites():
        for move in sends_of(ROUTES[r][0], dz, dx, dy):
            slots.setdefault((r, dx, dy, move), len(slots))
    return slots


def scan_down(x, rates):
    rows = x.shape[0]
    row = lax.broadcasted_iota(jnp.int32, x.shape, 0)
    step = 1
    while step < rows:
        factor = jnp.exp(-rates * float(step))
        if step < 8:
            moved = jnp.where(row >= step, pltpu.roll(x, step, 0), 0.0)
        else:
            moved = jnp.concatenate([jnp.zeros((step, x.shape[1]), F32), x[: rows - step]], axis=0)
        x = x + factor * moved
        step *= 2
    return x


def scan_up(x, rates):
    rows = x.shape[0]
    row = lax.broadcasted_iota(jnp.int32, x.shape, 0)
    step = 1
    while step < rows:
        factor = jnp.exp(-rates * float(step))
        if step < 8:
            moved = jnp.where(row < rows - step, pltpu.roll(x, rows - step, 0), 0.0)
        else:
            moved = jnp.concatenate([x[step:], jnp.zeros((step, x.shape[1]), F32)], axis=0)
        x = x + factor * moved
        step *= 2
    return x


def kernel(
    seq, gathers, docs_ref, q_ref, k_ref, v_ref, taps_ref, rates_ref, res_ref, skip_ref, w_ref, cot_ref,
    out_ref, gq_ref, gk_ref, gv_ref,
    wbuf, qs, ks, vs, conv, gated, acc, gqs, gp, edge, gsend, gedge, e_own, e_in, b_own, b_in,
    edge_sems, gedge_sems, e_sems, b_sems, local_sem, recv_sems, send_sems, core_sems, full_sems,
):
    me = lax.axis_index("seq")
    grp = lax.axis_index("groups")
    rows = q_ref.shape[0]
    chan = q_ref.shape[1]
    width = 256
    half_cols = cot_ref.shape[1] // 2
    piece_rows = w_ref.shape[0]
    per_dev = rows // BLOCK
    z, x, core = me // 4, (me // 2) % 2, me % 2

    starts = [jnp.int32(0)]
    for i in range(docs_ref.shape[0]):
        starts.append(starts[-1] + docs_ref[i])

    def free(low, high):
        kept = jnp.float32(1.0)
        for start in starts:
            kept = jnp.where((start >= low) & (start < high), 0.0, kept)
        return kept

    first = me * per_dev
    keep_0, keep_1, keep_n = free(first, first + 1), free(first + 1, first + 2), free(first + 2, first + 3)

    barrier = pltpu.get_barrier_semaphore()
    greeted = jnp.int32(0)
    for k in range(1, REACH + 1):
        for other in (me + k, me - k):
            there = (other >= 0) & (other < seq)

            @pl.when(there)
            def _():
                pl.semaphore_signal(barrier, inc=1, device_id=(grp, other), device_id_type=MESH_ID)

            greeted = greeted + there.astype(jnp.int32)
    if gathers:
        pl.semaphore_signal(barrier, inc=1, device_id=(1 - grp, me), device_id_type=MESH_ID)
        greeted = greeted + 1
    pl.semaphore_wait(barrier, greeted)

    def edge_copy(i, ref, target):
        return pltpu.make_async_remote_copy(
            src_ref=ref.at[pl.ds(rows - 16, 16)], dst_ref=edge.at[i], send_sem=edge_sems.at[i],
            recv_sem=edge_sems.at[3 + i], device_id=(grp, target), device_id_type=MESH_ID)

    @pl.when(me + 1 < seq)
    def _():
        for i, ref in enumerate((q_ref, k_ref, v_ref)):
            edge_copy(i, ref, me + 1).start()

    @pl.when(me == 0)
    def _():
        edge[...] = jnp.zeros_like(edge)

    offsets, at = [], 0
    for _, share in ROUTES:
        offsets.append((at * half_cols // 16, share * half_cols // 16))
        at += share
    slots = send_slots()

    def part(r, z_at, x_at, y_at, c_at):
        start, size = offsets[r]
        col = pl.multiple_of(y_at * half_cols + start, 128)
        return wbuf.at[z_at * 2 + x_at, pl.ds(pl.multiple_of(c_at * piece_rows, 16), piece_rows), pl.ds(col, size)]

    def own_rows(c_at):
        return wbuf.at[z * 2 + x, pl.ds(pl.multiple_of(c_at * piece_rows, 16), piece_rows)]

    def flat(r, dx, dy):
        return (r * 2 + dx) * 2 + dy

    def hop(r, z_at, dx, dy, move):
        ref = part(r, z_at, x ^ dx, grp ^ dy, core)
        to = {"up": (grp, me + 4), "down": (grp, me - 4), "x": (grp, me ^ 2), "y": (1 - grp, me)}[move]
        there = flat(r, dx ^ 1 if move == "x" else dx, dy ^ 1 if move == "y" else dy)
        return pltpu.make_async_remote_copy(
            src_ref=ref, dst_ref=ref, send_sem=send_sems.at[slots[(r, dx, dy, move)] * Z_SIZE + z_at],
            recv_sem=recv_sems.at[there * Z_SIZE + z_at], device_id=to, device_id_type=MESH_ID)

    def share_core(r, z_at, dx, dy, c_at):
        ref = part(r, z_at, x ^ dx, grp ^ dy, c_at)
        index = flat(r, dx, dy) * Z_SIZE + z_at
        return pltpu.make_async_remote_copy(
            src_ref=ref, dst_ref=ref, send_sem=core_sems.at[0, index], recv_sem=core_sems.at[1, index],
            device_id=(grp, me ^ 1), device_id_type=MESH_ID)

    def share_full(c_at):
        return pltpu.make_async_remote_copy(
            src_ref=own_rows(c_at), dst_ref=own_rows(c_at), send_sem=full_sems.at[0], recv_sem=full_sems.at[1],
            device_id=(grp, me ^ 1), device_id_type=MESH_ID)

    def when_valid(dz, action):
        z_at = z - dz
        if dz == 0:
            action(z)
        else:
            @pl.when((z_at >= 0) & (z_at < Z_SIZE))
            def _():
                action(z_at)

    def when_move(move, action):
        if move == "up":
            pl.when(z + 1 < Z_SIZE)(action)
        elif move == "down":
            pl.when(z > 0)(action)
        else:
            action()

    def visit(dz, dx, dy, r):
        def action(z_at):
            if dz != 0 or dx != 0:
                ref = part(r, z_at, x ^ dx, grp ^ dy, core)
                sem = recv_sems.at[flat(r, dx, dy) * Z_SIZE + z_at]
                pltpu.make_async_remote_copy(
                    src_ref=ref, dst_ref=ref, send_sem=sem, recv_sem=sem,
                    device_id=(grp, me ^ 1), device_id_type=MESH_ID).wait_recv()
            for move in sends_of(ROUTES[r][0], dz, dx, dy):
                when_move(move, lambda move=move: hop(r, z_at, dx, dy, move).start())
            if dz != 0 or dx != 0:
                share_core(r, z_at, dx, dy, core).start()
        when_valid(dz, action)

    sites = all_sites()
    if gathers:
        local = pltpu.make_async_copy(w_ref, own_rows(core), local_sem)
        local.start()
        local.wait()
        for _, dz, dx, dy, r in sites:
            if dz == 0 and dx == 0:
                visit(dz, dx, dy, r)
        share_full(core).start()
    else:
        local = pltpu.make_async_copy(w_ref, wbuf, local_sem)
        local.start()

    def columns(i):
        return pl.ds(pl.multiple_of(i * width, width), width)

    row = lax.broadcasted_iota(jnp.int32, (rows, width), 0)
    block_row = lax.broadcasted_iota(jnp.int32, (BLOCK, width), 0).astype(F32)

    def weights_of(cols):
        rates = rates_ref[:, cols]
        return rates, res_ref[:, cols] * jnp.sqrt(2.0 * rates)

    lag_1 = jnp.where(row == 0, keep_0, jnp.where(row == BLOCK, keep_1, 1.0))
    lag_2 = jnp.where(row < 2, keep_0, jnp.where((row == BLOCK) | (row == BLOCK + 1), keep_1, 1.0))

    @pl.when(me > 0)
    def _():
        for i, ref in enumerate((q_ref, k_ref, v_ref)):
            edge_copy(i, ref, me).wait_recv()

    def forward_chunk(i, carry):
        cols = columns(i)

        def short(b, ref):
            now = ref[:, cols].astype(F32)
            before = edge[b, :, cols].astype(F32)
            one = jnp.where(row == 0, before[15:16], pltpu.roll(now, 1, 0))
            two = jnp.where(row == 0, before[14:15], jnp.where(row == 1, before[15:16], pltpu.roll(now, 2, 0)))
            return (taps_ref[b, 0:1, cols] * now + taps_ref[b, 1:2, cols] * (lag_1 * one)
                    + taps_ref[b, 2:3, cols] * (lag_2 * two))

        qs[:, cols] = short(0, q_ref)
        k_now, v_now = short(1, k_ref), short(2, v_ref)
        ks[:, cols] = k_now
        vs[:, cols] = v_now
        product = k_now * v_now
        rates, weight = weights_of(cols)
        skip = skip_ref[:, cols]
        top, low = skip * product[:BLOCK], skip * product[BLOCK:]
        for m in range(2):
            rate = rates[m : m + 1]
            y_0 = scan_down(product[:BLOCK], rate)
            y_1 = scan_down(product[BLOCK:], rate)
            y_1 = y_1 + jnp.exp(-rate * (block_row + 1.0)) * (keep_1 * y_0[BLOCK - 1 :])
            e_own[m : m + 1, cols] = y_1[BLOCK - 1 :]
            top = top + weight[m : m + 1] * y_0
            low = low + weight[m : m + 1] * y_1
        conv[:BLOCK, cols] = top
        conv[BLOCK:, cols] = low
        return carry

    lax.fori_loop(0, chan // width, forward_chunk, 0)

    def state_copy(own, into, sems, k, target):
        return pltpu.make_async_remote_copy(
            src_ref=own, dst_ref=into.at[k - 1], send_sem=sems.at[0, k - 1], recv_sem=sems.at[1, k - 1],
            device_id=(grp, target), device_id_type=MESH_ID)

    def send_states(own, into, sems, sign):
        for k in range(1, REACH + 1):
            @pl.when((me + sign * k >= 0) & (me + sign * k < seq))
            def _():
                state_copy(own, into, sems, k, me + sign * k).start()

    def take_states(own, into, sems, sign):
        for k in range(1, REACH + 1):
            there = (me - sign * k >= 0) & (me - sign * k < seq)

            @pl.when(there)
            def _():
                state_copy(own, into, sems, k, me).wait_recv()

            @pl.when(jnp.logical_not(there))
            def _():
                into[k - 1] = jnp.zeros_like(into[k - 1])

    def joined(into, rates, cols, kept):
        total = jnp.zeros_like(rates)
        for k in range(1, REACH + 1):
            total = total + into[k - 1, :, cols] * jnp.exp(-rates * float(rows * (k - 1))) * kept[k - 1]
        return total

    send_states(e_own, e_in, e_sems, 1)
    if gathers:
        for level, dz, dx, dy, r in sites:
            if level == 1 and (dz != 0 or dx != 0):
                visit(dz, dx, dy, r)
    take_states(e_own, e_in, e_sems, 1)
    kept_f = [free(per_dev * (me - k + 1), first) for k in range(1, REACH + 1)]
    kept_b = [free(first + per_dev + 1, first + per_dev * k + 1) for k in range(1, REACH + 1)]

    def forward_finish(i, carry):
        cols = columns(i)
        rates, weight = weights_of(cols)
        ahead = joined(e_in, rates, cols, kept_f) * weight * keep_0
        later = ahead * keep_1 * jnp.exp(-rates * float(BLOCK))
        top, low = conv[:BLOCK, cols], conv[BLOCK:, cols]
        for m in range(2):
            power = jnp.exp(-rates[m : m + 1] * (block_row + 1.0))
            top = top + power * ahead[m : m + 1]
            low = low + power * later[m : m + 1]
        conv[:BLOCK, cols] = top
        conv[BLOCK:, cols] = low
        gated[:BLOCK, cols] = (qs[:BLOCK, cols] * top).astype(BF16)
        gated[BLOCK:, cols] = (qs[BLOCK:, cols] * low).astype(BF16)
        return carry

    lax.fori_loop(0, chan // width, forward_finish, 0)
    acc[...] = jnp.zeros_like(acc)

    tile = 512

    def multiply(j):
        cols = columns(j)
        grad = lax.dot_general(cot_ref[...], wbuf[j], (((1,), (1,)), ((), ())), preferred_element_type=F32)
        gqs[:, cols] = grad * conv[:, cols]
        grad_conv = grad * qs[:, cols]
        rates, weight = weights_of(cols)
        skip = skip_ref[:, cols]
        top, low = skip * grad_conv[:BLOCK], skip * grad_conv[BLOCK:]
        for m in range(2):
            rate = rates[m : m + 1]
            y_0 = scan_up(grad_conv[:BLOCK], rate)
            y_1 = scan_up(grad_conv[BLOCK:], rate)
            y_0 = y_0 + jnp.exp(-rate * (BLOCK - block_row)) * (keep_1 * y_1[0:1])
            b_own[m : m + 1, cols] = y_0[0:1]
            top = top + weight[m : m + 1] * y_0
            low = low + weight[m : m + 1] * y_1
        gp[:BLOCK, cols] = top
        gp[BLOCK:, cols] = low

        def mixed(t, carry):
            at = pl.ds(pl.multiple_of(t * tile, tile), tile)
            acc[:, at] = acc[:, at] + jnp.dot(gated[:, cols], wbuf[j, :, at], preferred_element_type=F32)
            return carry

        lax.fori_loop(0, acc.shape[1] // tile, mixed, 0)

    def settle(dz, dx):
        def action(z_at):
            if dz == 0 and dx == 0:
                share_full(1 - core).wait_recv()
            else:
                for dy in range(2):
                    for r in range(len(ROUTES)):
                        share_core(r, z_at, dx, dy, 1 - core).wait_recv()
            multiply(z_at * 2 + (x ^ dx))
        when_valid(dz, action)

    if gathers:
        top_level = max(site[0] for site in sites)
        pairs = sorted((abs(dz) + dx + 1, dz, dx) for dz in range(1 - Z_SIZE, Z_SIZE) for dx in range(2))
        for level in range(2, top_level + 2):
            for site_level, dz, dx, dy, r in sites:
                if site_level == level and (dz != 0 or dx != 0):
                    visit(dz, dx, dy, r)
            for pair_level, dz, dx in pairs:
                if pair_level == level - 1:
                    settle(dz, dx)
        for pair_level, dz, dx in pairs:
            if pair_level > top_level:
                settle(dz, dx)
    else:
        local.wait()

        def each(j, carry):
            multiply(j)
            return carry

        lax.fori_loop(0, chan // width, each, 0)

    send_states(b_own, b_in, b_sems, -1)

    def write_mixed(t, carry):
        at = pl.ds(pl.multiple_of(t * tile, tile), tile)
        out_ref[:, at] = acc[:, at].astype(BF16)
        return carry

    lax.fori_loop(0, acc.shape[1] // tile, write_mixed, 0)
    take_states(b_own, b_in, b_sems, -1)

    def backward_finish(i, carry):
        cols = columns(i)
        rates, weight = weights_of(cols)
        behind = joined(b_in, rates, cols, kept_b) * weight * keep_n
        sooner = behind * keep_1 * jnp.exp(-rates * float(BLOCK))
        top, low = gp[:BLOCK, cols], gp[BLOCK:, cols]
        for m in range(2):
            power = jnp.exp(-rates[m : m + 1] * (BLOCK - block_row))
            top = top + power * sooner[m : m + 1]
            low = low + power * behind[m : m + 1]
        grad = jnp.concatenate([top, low], axis=0)
        k_now = ks[:, cols]
        grad_k, grad_v = grad * vs[:, cols], grad * k_now
        ks[:, cols] = grad_k
        vs[:, cols] = grad_v
        gsend[0, :, cols] = gqs[0:8, cols]
        gsend[1, :, cols] = grad_k[0:8]
        gsend[2, :, cols] = grad_v[0:8]
        return carry

    lax.fori_loop(0, chan // width, backward_finish, 0)

    def gedge_copy(target):
        return pltpu.make_async_remote_copy(
            src_ref=gsend, dst_ref=gedge, send_sem=gedge_sems.at[0], recv_sem=gedge_sems.at[1],
            device_id=(grp, target), device_id_type=MESH_ID)

    @pl.when(me > 0)
    def _():
        gedge_copy(me - 1).start()

    @pl.when(me == seq - 1)
    def _():
        gedge[...] = jnp.zeros_like(gedge)

    @pl.when(me + 1 < seq)
    def _():
        gedge_copy(me).wait_recv()

    lead_1 = jnp.where(row == BLOCK - 1, keep_1, jnp.where(row == rows - 1, keep_n, 1.0))
    lead_2 = jnp.where((row == BLOCK - 1) | (row == BLOCK - 2), keep_1, jnp.where(row >= rows - 2, keep_n, 1.0))

    def backward_short(i, carry):
        cols = columns(i)
        for b, (grad_ref, to_ref) in enumerate(((gqs, gq_ref), (ks, gk_ref), (vs, gv_ref))):
            now = grad_ref[:, cols]
            after = gedge[b, :, cols]
            one = jnp.where(row == rows - 1, after[0:1], pltpu.roll(now, rows - 1, 0))
            two = jnp.where(row == rows - 1, after[1:2],
                            jnp.where(row == rows - 2, after[0:1], pltpu.roll(now, rows - 2, 0)))
            to_ref[:, cols] = (taps_ref[b, 0:1, cols] * now + taps_ref[b, 1:2, cols] * (lead_1 * one)
                               + taps_ref[b, 2:3, cols] * (lead_2 * two)).astype(BF16)
        return carry

    lax.fori_loop(0, chan // width, backward_short, 0)

    @pl.when(me + 1 < seq)
    def _():
        for i, ref in enumerate((q_ref, k_ref, v_ref)):
            edge_copy(i, ref, me + 1).wait_send()

    @pl.when(me > 0)
    def _():
        gedge_copy(me - 1).wait_send()

    for own, into, sems, sign in ((e_own, e_in, e_sems, 1), (b_own, b_in, b_sems, -1)):
        for k in range(1, REACH + 1):
            @pl.when((me + sign * k >= 0) & (me + sign * k < seq))
            def _():
                state_copy(own, into, sems, k, me + sign * k).wait_send()

    if gathers:
        share_full(core).wait_send()
        for _, dz, dx, dy, r in sites:
            def action(z_at):
                for move in sends_of(ROUTES[r][0], dz, dx, dy):
                    when_move(move, lambda move=move: hop(r, z_at, dx, dy, move).wait_send())
                if dz != 0 or dx != 0:
                    share_core(r, z_at, dx, dy, core).wait_send()
            when_valid(dz, action)


def on_device(queries, key_inputs, values, short_taps, decay_rates, residues, skip_gain, out_weight, cotangent,
              doc_blocks):
    seq = lax.axis_size("seq")
    rows, chan = queries.shape
    model = out_weight.shape[1]
    gathers = seq == 4 * Z_SIZE and lax.axis_size("groups") == 2
    pairs = chan // 256
    if not gathers:
        out_weight = lax.all_gather(out_weight, "seq", axis=0, tiled=True).reshape(pairs, 256, model)
    vmem = pl.BlockSpec(memory_space=pltpu.VMEM)
    dma = pltpu.SemaphoreType.DMA
    count = len(ROUTES) * 4 * Z_SIZE
    full = (rows, chan)
    return pl.pallas_call(
        functools.partial(kernel, seq, gathers),
        out_shape=(
            jax.ShapeDtypeStruct((rows, model), BF16),
            jax.ShapeDtypeStruct(full, BF16),
            jax.ShapeDtypeStruct(full, BF16),
            jax.ShapeDtypeStruct(full, BF16),
        ),
        in_specs=[pl.BlockSpec(memory_space=pltpu.SMEM)] + [vmem] * 7
        + [pl.BlockSpec(memory_space=pl.ANY)] + [vmem],
        out_specs=(vmem,) * 4,
        scratch_shapes=[
            pltpu.VMEM((pairs, 256, model), BF16),
            pltpu.VMEM(full, F32), pltpu.VMEM(full, F32), pltpu.VMEM(full, F32), pltpu.VMEM(full, F32),
            pltpu.VMEM(full, BF16),
            pltpu.VMEM((rows, model), F32),
            pltpu.VMEM(full, F32), pltpu.VMEM(full, F32),
            pltpu.VMEM((3, 16, chan), BF16),
            pltpu.VMEM((3, 8, chan), F32), pltpu.VMEM((3, 8, chan), F32),
            pltpu.VMEM((2, chan), F32), pltpu.VMEM((REACH, 2, chan), F32),
            pltpu.VMEM((2, chan), F32), pltpu.VMEM((REACH, 2, chan), F32),
            dma((6,)), dma((2,)), dma((2, REACH)), dma((2, REACH)), dma,
            dma((count,)), dma((len(send_slots()) * Z_SIZE,)), dma((2, count)), dma((2,)),
        ],
        compiler_params=pltpu.CompilerParams(
            collective_id=0, has_side_effects=True, vmem_limit_bytes=60 * 1024 * 1024),
    )(doc_blocks, queries, key_inputs, values, short_taps, decay_rates, residues, skip_gain.reshape(1, chan),
      out_weight, cotangent)


def solution(mesh):
    rows = P(("groups", "seq"), None)
    return jax.shard_map(
        on_device,
        mesh=mesh,
        in_specs=(rows, rows, rows, P(), P(), P(), P(), P("seq", None), rows, P("groups")),
        out_specs=(rows, rows, rows, rows),
        check_vma=False,
    )
```

```python
import functools

import jax
import jax.numpy as jnp
from jax import lax
from jax.experimental import pallas as pl
from jax.experimental.pallas import tpu as pltpu
from jax.sharding import PartitionSpec as P

BLOCK = 128
REACH = 8
Z_SIZE = 4
MESH_ID = pl.DeviceIdType.MESH
ROUTES = (("zxy", 7), ("zyx", 6), ("xyz", 3))
F32 = jnp.float32
BF16 = jnp.bfloat16


def last_axis(order, dz, dx, dy):
    moved = {"z": dz != 0, "x": dx != 0, "y": dy != 0}
    if dz == 0 and dx == 0:
        return -1 if dy == 0 else order.index("y")
    return max(i for i in range(3) if moved[order[i]])


def sends_of(order, dz, dx, dy):
    last = last_axis(order, dz, dx, dy)
    moves = []
    for i in range(3):
        axis = order[i]
        if i < last or (i == last and axis != "z"):
            continue
        if axis == "z":
            if dz >= 0:
                moves.append("up")
            if dz <= 0:
                moves.append("down")
        elif axis == "x":
            moves.append("x")
        elif not (dz == 0 and dx == 0):
            moves.append("y")
    return moves


def all_sites():
    sites = []
    for dz in range(-(Z_SIZE - 1), Z_SIZE):
        for dx in range(2):
            for dy in range(2):
                for r in range(len(ROUTES)):
                    sites.append((abs(dz) + dx + dy, dz, dx, dy, r))
    return sorted(sites)


def send_slots():
    slots = {}
    for _, dz, dx, dy, r in all_sites():
        for move in sends_of(ROUTES[r][0], dz, dx, dy):
            slots.setdefault((r, dx, dy, move), len(slots))
    return slots


def scan_down(x, rates):
    rows = x.shape[0]
    row = lax.broadcasted_iota(jnp.int32, x.shape, 0)
    step = 1
    while step < rows:
        factor = jnp.exp(-rates * float(step))
        if step < 8:
            moved = jnp.where(row >= step, pltpu.roll(x, step, 0), 0.0)
        else:
            moved = jnp.concatenate([jnp.zeros((step, x.shape[1]), F32), x[: rows - step]], axis=0)
        x = x + factor * moved
        step *= 2
    return x


def scan_up(x, rates):
    rows = x.shape[0]
    row = lax.broadcasted_iota(jnp.int32, x.shape, 0)
    step = 1
    while step < rows:
        factor = jnp.exp(-rates * float(step))
        if step < 8:
            moved = jnp.where(row < rows - step, pltpu.roll(x, rows - step, 0), 0.0)
        else:
            moved = jnp.concatenate([x[step:], jnp.zeros((step, x.shape[1]), F32)], axis=0)
        x = x + factor * moved
        step *= 2
    return x


def kernel(
    seq, gathers, docs_ref, q_hbm, k_hbm, v_hbm, taps_ref, rates_ref, res_ref, skip_ref, w_ref, cot_hbm,
    out_hbm, gq_hbm, gk_hbm, gv_hbm,
    q_ref, k_ref, v_ref, cot_ref, out_ref, gq_ref, gk_ref, gv_ref,
    wbuf, qs, ks, vs, conv, gated, acc, gqs, gp, edge, gsend, gedge, e_own, e_in, b_own, b_in,
    edge_sems, gedge_sems, e_sems, b_sems, local_sem, recv_sems, send_sems, core_sems, full_sems, in_sems, out_sems,
):
    me = lax.axis_index("seq")
    grp = lax.axis_index("groups")
    rows = q_ref.shape[0]
    chan = q_ref.shape[1]
    width = 256
    half_cols = cot_ref.shape[1] // 2
    piece_rows = w_ref.shape[0]
    per_dev = rows // BLOCK
    z, x, core = me // 4, (me // 2) % 2, me % 2

    starts = [jnp.int32(0)]
    for i in range(docs_ref.shape[0]):
        starts.append(starts[-1] + docs_ref[i])

    def free(low, high):
        kept = jnp.float32(1.0)
        for start in starts:
            kept = jnp.where((start >= low) & (start < high), 0.0, kept)
        return kept

    first = me * per_dev
    keep_0, keep_1, keep_n = free(first, first + 1), free(first + 1, first + 2), free(first + 2, first + 3)

    loads = [pltpu.make_async_copy(a, b, in_sems.at[i]) for i, (a, b) in enumerate(
        ((q_hbm, q_ref), (k_hbm, k_ref), (v_hbm, v_ref), (cot_hbm, cot_ref)))]
    for load in loads:
        load.start()

    barrier = pltpu.get_barrier_semaphore()
    greeted = jnp.int32(0)
    for k in range(1, REACH + 1):
        for other in (me + k, me - k):
            there = (other >= 0) & (other < seq)

            @pl.when(there)
            def _():
                pl.semaphore_signal(barrier, inc=1, device_id=(grp, other), device_id_type=MESH_ID)

            greeted = greeted + there.astype(jnp.int32)
    if gathers:
        pl.semaphore_signal(barrier, inc=1, device_id=(1 - grp, me), device_id_type=MESH_ID)
        greeted = greeted + 1
    pl.semaphore_wait(barrier, greeted)

    def edge_copy(i, ref, target):
        return pltpu.make_async_remote_copy(
            src_ref=ref.at[pl.ds(rows - 16, 16)], dst_ref=edge.at[i], send_sem=edge_sems.at[i],
            recv_sem=edge_sems.at[3 + i], device_id=(grp, target), device_id_type=MESH_ID)

    offsets, at = [], 0
    for _, share in ROUTES:
        offsets.append((at * half_cols // 16, share * half_cols // 16))
        at += share
    slots = send_slots()

    def part(r, z_at, x_at, y_at, c_at):
        start, size = offsets[r]
        col = pl.multiple_of(y_at * half_cols + start, 128)
        return wbuf.at[z_at * 2 + x_at, pl.ds(pl.multiple_of(c_at * piece_rows, 16), piece_rows), pl.ds(col, size)]

    def own_rows(c_at):
        return wbuf.at[z * 2 + x, pl.ds(pl.multiple_of(c_at * piece_rows, 16), piece_rows)]

    def flat(r, dx, dy):
        return (r * 2 + dx) * 2 + dy

    def hop(r, z_at, dx, dy, move, own):
        ref = part(r, z_at, x ^ dx, grp ^ dy, core)
        source = ref
        if own:
            start, size = offsets[r]
            source = w_ref.at[:, pl.ds(pl.multiple_of((grp ^ dy) * half_cols + start, 128), size)]
        to = {"up": (grp, me + 4), "down": (grp, me - 4), "x": (grp, me ^ 2), "y": (1 - grp, me)}[move]
        there = flat(r, dx ^ 1 if move == "x" else dx, dy ^ 1 if move == "y" else dy)
        return pltpu.make_async_remote_copy(
            src_ref=source, dst_ref=ref, send_sem=send_sems.at[slots[(r, dx, dy, move)] * Z_SIZE + z_at],
            recv_sem=recv_sems.at[there * Z_SIZE + z_at], device_id=to, device_id_type=MESH_ID)

    def share_core(r, z_at, dx, dy, c_at):
        ref = part(r, z_at, x ^ dx, grp ^ dy, c_at)
        index = flat(r, dx, dy) * Z_SIZE + z_at
        return pltpu.make_async_remote_copy(
            src_ref=ref, dst_ref=ref, send_sem=core_sems.at[0, index], recv_sem=core_sems.at[1, index],
            device_id=(grp, me ^ 1), device_id_type=MESH_ID)

    def share_full(c_at):
        return pltpu.make_async_remote_copy(
            src_ref=w_ref, dst_ref=own_rows(c_at), send_sem=full_sems.at[0], recv_sem=full_sems.at[1],
            device_id=(grp, me ^ 1), device_id_type=MESH_ID)

    def when_valid(dz, action):
        z_at = z - dz
        if dz == 0:
            action(z)
        else:
            @pl.when((z_at >= 0) & (z_at < Z_SIZE))
            def _():
                action(z_at)

    def when_move(move, action):
        if move == "up":
            pl.when(z + 1 < Z_SIZE)(action)
        elif move == "down":
            pl.when(z > 0)(action)
        else:
            action()

    def visit(dz, dx, dy, r):
        def action(z_at):
            if dz != 0 or dx != 0:
                ref = part(r, z_at, x ^ dx, grp ^ dy, core)
                sem = recv_sems.at[flat(r, dx, dy) * Z_SIZE + z_at]
                pltpu.make_async_remote_copy(
                    src_ref=ref, dst_ref=ref, send_sem=sem, recv_sem=sem,
                    device_id=(grp, me ^ 1), device_id_type=MESH_ID).wait_recv()
            for move in sends_of(ROUTES[r][0], dz, dx, dy):
                when_move(move, lambda move=move: hop(r, z_at, dx, dy, move, dz == 0 and dx == 0).start())
            if dz != 0 or dx != 0:
                share_core(r, z_at, dx, dy, core).start()
        when_valid(dz, action)

    sites = all_sites()
    if gathers:
        local = pltpu.make_async_copy(w_ref, own_rows(core), local_sem)
        local.start()
        for _, dz, dx, dy, r in sites:
            if dz == 0 and dx == 0:
                visit(dz, dx, dy, r)
        share_full(core).start()
    else:
        local = pltpu.make_async_copy(w_ref, wbuf, local_sem)
        local.start()

    for load in loads[:3]:
        load.wait()

    @pl.when(me + 1 < seq)
    def _():
        for i, ref in enumerate((q_ref, k_ref, v_ref)):
            edge_copy(i, ref, me + 1).start()

    @pl.when(me == 0)
    def _():
        edge[...] = jnp.zeros_like(edge)

    def columns(i):
        return pl.ds(pl.multiple_of(i * width, width), width)

    row = lax.broadcasted_iota(jnp.int32, (rows, width), 0)
    block_row = lax.broadcasted_iota(jnp.int32, (BLOCK, width), 0).astype(F32)

    def weights_of(cols):
        rates = rates_ref[:, cols]
        return rates, res_ref[:, cols] * jnp.sqrt(2.0 * rates)

    lag_1 = jnp.where(row == 0, keep_0, jnp.where(row == BLOCK, keep_1, 1.0))
    lag_2 = jnp.where(row < 2, keep_0, jnp.where((row == BLOCK) | (row == BLOCK + 1), keep_1, 1.0))

    @pl.when(me > 0)
    def _():
        for i, ref in enumerate((q_ref, k_ref, v_ref)):
            edge_copy(i, ref, me).wait_recv()

    def forward_chunk(i, carry):
        cols = columns(i)

        def short(b, ref):
            now = ref[:, cols].astype(F32)
            before = edge[b, :, cols].astype(F32)
            one = jnp.where(row == 0, before[15:16], pltpu.roll(now, 1, 0))
            two = jnp.where(row == 0, before[14:15], jnp.where(row == 1, before[15:16], pltpu.roll(now, 2, 0)))
            return (taps_ref[b, 0:1, cols] * now + taps_ref[b, 1:2, cols] * (lag_1 * one)
                    + taps_ref[b, 2:3, cols] * (lag_2 * two))

        qs[:, cols] = short(0, q_ref)
        k_now, v_now = short(1, k_ref), short(2, v_ref)
        ks[:, cols] = k_now
        vs[:, cols] = v_now
        product = k_now * v_now
        rates, weight = weights_of(cols)
        skip = skip_ref[:, cols]
        top, low = skip * product[:BLOCK], skip * product[BLOCK:]
        for m in range(2):
            rate = rates[m : m + 1]
            y_0 = scan_down(product[:BLOCK], rate)
            y_1 = scan_down(product[BLOCK:], rate)
            y_1 = y_1 + jnp.exp(-rate * (block_row + 1.0)) * (keep_1 * y_0[BLOCK - 1 :])
            e_own[m : m + 1, cols] = y_1[BLOCK - 1 :]
            top = top + weight[m : m + 1] * y_0
            low = low + weight[m : m + 1] * y_1
        conv[:BLOCK, cols] = top
        conv[BLOCK:, cols] = low
        return carry

    quarter = chan // width // 4
    for turn in range(4):
        lax.fori_loop(turn * quarter, (turn + 1) * quarter, forward_chunk, 0)
        if gathers and turn > 0:
            for level, dz, dx, dy, r in sites:
                if level == 1 and (abs(dz), dx, dy) == ((1, 0, 0), (0, 1, 0), (9, 9, 9))[turn - 1]:
                    visit(dz, dx, dy, r)

    def state_copy(own, into, sems, k, target):
        return pltpu.make_async_remote_copy(
            src_ref=own, dst_ref=into.at[k - 1], send_sem=sems.at[0, k - 1], recv_sem=sems.at[1, k - 1],
            device_id=(grp, target), device_id_type=MESH_ID)

    def send_states(own, into, sems, sign):
        for k in range(1, REACH + 1):
            @pl.when((me + sign * k >= 0) & (me + sign * k < seq))
            def _():
                state_copy(own, into, sems, k, me + sign * k).start()

    def take_states(own, into, sems, sign):
        for k in range(1, REACH + 1):
            there = (me - sign * k >= 0) & (me - sign * k < seq)

            @pl.when(there)
            def _():
                state_copy(own, into, sems, k, me).wait_recv()

            @pl.when(jnp.logical_not(there))
            def _():
                into[k - 1] = jnp.zeros_like(into[k - 1])

    def joined(into, rates, cols, kept):
        total = jnp.zeros_like(rates)
        for k in range(1, REACH + 1):
            total = total + into[k - 1, :, cols] * jnp.exp(-rates * float(rows * (k - 1))) * kept[k - 1]
        return total

    send_states(e_own, e_in, e_sems, 1)
    take_states(e_own, e_in, e_sems, 1)
    kept_f = [free(per_dev * (me - k + 1), first) for k in range(1, REACH + 1)]
    kept_b = [free(first + per_dev + 1, first + per_dev * k + 1) for k in range(1, REACH + 1)]

    def forward_finish(i, carry):
        cols = columns(i)
        rates, weight = weights_of(cols)
        ahead = joined(e_in, rates, cols, kept_f) * weight * keep_0
        later = ahead * keep_1 * jnp.exp(-rates * float(BLOCK))
        top, low = conv[:BLOCK, cols], conv[BLOCK:, cols]
        for m in range(2):
            power = jnp.exp(-rates[m : m + 1] * (block_row + 1.0))
            top = top + power * ahead[m : m + 1]
            low = low + power * later[m : m + 1]
        conv[:BLOCK, cols] = top
        conv[BLOCK:, cols] = low
        gated[:BLOCK, cols] = (qs[:BLOCK, cols] * top).astype(BF16)
        gated[BLOCK:, cols] = (qs[BLOCK:, cols] * low).astype(BF16)
        return carry

    lax.fori_loop(0, chan // width, forward_finish, 0)
    acc[...] = jnp.zeros_like(acc)
    loads[3].wait()

    tile = 512

    def multiply(j):
        cols = columns(j)
        grad = lax.dot_general(cot_ref[...], wbuf[j], (((1,), (1,)), ((), ())), preferred_element_type=F32)
        gqs[:, cols] = grad * conv[:, cols]
        grad_conv = grad * qs[:, cols]
        rates, weight = weights_of(cols)
        skip = skip_ref[:, cols]
        top, low = skip * grad_conv[:BLOCK], skip * grad_conv[BLOCK:]
        for m in range(2):
            rate = rates[m : m + 1]
            y_0 = scan_up(grad_conv[:BLOCK], rate)
            y_1 = scan_up(grad_conv[BLOCK:], rate)
            y_0 = y_0 + jnp.exp(-rate * (BLOCK - block_row)) * (keep_1 * y_1[0:1])
            b_own[m : m + 1, cols] = y_0[0:1]
            top = top + weight[m : m + 1] * y_0
            low = low + weight[m : m + 1] * y_1
        gp[:BLOCK, cols] = top
        gp[BLOCK:, cols] = low

        def mixed(t, carry):
            at = pl.ds(pl.multiple_of(t * tile, tile), tile)
            acc[:, at] = acc[:, at] + jnp.dot(gated[:, cols], wbuf[j, :, at], preferred_element_type=F32)
            return carry

        lax.fori_loop(0, acc.shape[1] // tile, mixed, 0, unroll=8)

    def settle(dz, dx):
        def action(z_at):
            if dz == 0 and dx == 0:
                local.wait()
                share_full(1 - core).wait_recv()
            else:
                for dy in range(2):
                    for r in range(len(ROUTES)):
                        share_core(r, z_at, dx, dy, 1 - core).wait_recv()
            multiply(z_at * 2 + (x ^ dx))
        when_valid(dz, action)

    if gathers:
        top_level = max(site[0] for site in sites)
        pairs = sorted((abs(dz) + dx + 1, dz, dx) for dz in range(1 - Z_SIZE, Z_SIZE) for dx in range(2))
        for level in range(2, top_level + 2):
            ready = [pair[1:] for pair in pairs if pair[0] == level - 1]
            groups = sorted({site[1:4] for site in sites if site[0] == level and (site[1] != 0 or site[2] != 0)},
                            key=lambda at: (at[2], at[1], at[0]))
            for count, at in enumerate(groups):
                for r in range(len(ROUTES)):
                    visit(*at, r)
                if count % 2 == 1 and ready:
                    settle(*ready.pop(0))
            for pair in ready:
                settle(*pair)
        for pair_level, dz, dx in pairs:
            if pair_level > top_level:
                settle(dz, dx)
    else:
        local.wait()

        def each(j, carry):
            multiply(j)
            return carry

        lax.fori_loop(0, chan // width, each, 0)

    send_states(b_own, b_in, b_sems, -1)

    def write_mixed(t, carry):
        at = pl.ds(pl.multiple_of(t * tile, tile), tile)
        out_ref[:, at] = acc[:, at].astype(BF16)
        return carry

    lax.fori_loop(0, acc.shape[1] // tile, write_mixed, 0)
    stores = [pltpu.make_async_copy(a, b, out_sems.at[i]) for i, (a, b) in enumerate(
        ((out_ref, out_hbm), (gq_ref, gq_hbm), (gk_ref, gk_hbm), (gv_ref, gv_hbm)))]
    stores[0].start()
    take_states(b_own, b_in, b_sems, -1)

    def backward_finish(i, carry):
        cols = columns(i)
        rates, weight = weights_of(cols)
        behind = joined(b_in, rates, cols, kept_b) * weight * keep_n
        sooner = behind * keep_1 * jnp.exp(-rates * float(BLOCK))
        top, low = gp[:BLOCK, cols], gp[BLOCK:, cols]
        for m in range(2):
            power = jnp.exp(-rates[m : m + 1] * (BLOCK - block_row))
            top = top + power * sooner[m : m + 1]
            low = low + power * behind[m : m + 1]
        grad = jnp.concatenate([top, low], axis=0)
        k_now = ks[:, cols]
        grad_k, grad_v = grad * vs[:, cols], grad * k_now
        ks[:, cols] = grad_k
        vs[:, cols] = grad_v
        gsend[0, :, cols] = gqs[0:8, cols]
        gsend[1, :, cols] = grad_k[0:8]
        gsend[2, :, cols] = grad_v[0:8]
        return carry

    lax.fori_loop(0, chan // width, backward_finish, 0)

    def gedge_copy(target):
        return pltpu.make_async_remote_copy(
            src_ref=gsend, dst_ref=gedge, send_sem=gedge_sems.at[0], recv_sem=gedge_sems.at[1],
            device_id=(grp, target), device_id_type=MESH_ID)

    @pl.when(me > 0)
    def _():
        gedge_copy(me - 1).start()

    @pl.when(me == seq - 1)
    def _():
        gedge[...] = jnp.zeros_like(gedge)

    @pl.when(me + 1 < seq)
    def _():
        gedge_copy(me).wait_recv()

    lead_1 = jnp.where(row == BLOCK - 1, keep_1, jnp.where(row == rows - 1, keep_n, 1.0))
    lead_2 = jnp.where((row == BLOCK - 1) | (row == BLOCK - 2), keep_1, jnp.where(row >= rows - 2, keep_n, 1.0))

    def backward_short(i, carry):
        cols = columns(i)
        for b, (grad_ref, to_ref) in enumerate(((gqs, gq_ref), (ks, gk_ref), (vs, gv_ref))):
            now = grad_ref[:, cols]
            after = gedge[b, :, cols]
            one = jnp.where(row == rows - 1, after[0:1], pltpu.roll(now, rows - 1, 0))
            two = jnp.where(row == rows - 1, after[1:2],
                            jnp.where(row == rows - 2, after[0:1], pltpu.roll(now, rows - 2, 0)))
            to_ref[:, cols] = (taps_ref[b, 0:1, cols] * now + taps_ref[b, 1:2, cols] * (lead_1 * one)
                               + taps_ref[b, 2:3, cols] * (lead_2 * two)).astype(BF16)
        return carry

    lax.fori_loop(0, chan // width, backward_short, 0)

    for store in stores[1:]:
        store.start()

    @pl.when(me + 1 < seq)
    def _():
        for i, ref in enumerate((q_ref, k_ref, v_ref)):
            edge_copy(i, ref, me + 1).wait_send()

    @pl.when(me > 0)
    def _():
        gedge_copy(me - 1).wait_send()

    for own, into, sems, sign in ((e_own, e_in, e_sems, 1), (b_own, b_in, b_sems, -1)):
        for k in range(1, REACH + 1):
            @pl.when((me + sign * k >= 0) & (me + sign * k < seq))
            def _():
                state_copy(own, into, sems, k, me + sign * k).wait_send()

    if gathers:
        share_full(core).wait_send()
        for _, dz, dx, dy, r in sites:
            def action(z_at):
                for move in sends_of(ROUTES[r][0], dz, dx, dy):
                    when_move(move, lambda move=move: hop(r, z_at, dx, dy, move, dz == 0 and dx == 0).wait_send())
                if dz != 0 or dx != 0:
                    share_core(r, z_at, dx, dy, core).wait_send()
            when_valid(dz, action)

    for store in stores:
        store.wait()


def hand_on(*refs):
    count = (len(refs) - 2) // 3
    sems, back_sems = refs[-2:]
    takes, gives = [], []
    for i in range(count):
        rows = refs[i].shape[0] // 4
        for t in range(4):
            at = pl.ds(t * rows, rows)
            held = refs[2 * count + i].at[at]
            takes.append(pltpu.make_async_copy(refs[i].at[at], held, sems.at[i * 4 + t]))
            gives.append(pltpu.make_async_copy(held, refs[count + i].at[at], back_sems.at[i * 4 + t]))
    for take in takes:
        take.start()
    for take, give in zip(takes, gives):
        take.wait()
        give.start()
    for give in gives:
        give.wait()


def on_device(queries, key_inputs, values, short_taps, decay_rates, residues, skip_gain, out_weight, cotangent,
              doc_blocks):
    seq = lax.axis_size("seq")
    rows, chan = queries.shape
    model = out_weight.shape[1]
    gathers = seq == 4 * Z_SIZE and lax.axis_size("groups") == 2
    pairs = chan // 256
    if not gathers:
        out_weight = lax.all_gather(out_weight, "seq", axis=0, tiled=True).reshape(pairs, 256, model)
    vmem = pl.BlockSpec(memory_space=pltpu.VMEM)
    dma = pltpu.SemaphoreType.DMA
    count = len(ROUTES) * 4 * Z_SIZE
    full = (rows, chan)
    anywhere = pl.BlockSpec(memory_space=pl.ANY)
    outs = pl.pallas_call(
        functools.partial(kernel, seq, gathers),
        out_shape=(
            jax.ShapeDtypeStruct((rows, model), BF16),
            jax.ShapeDtypeStruct(full, BF16),
            jax.ShapeDtypeStruct(full, BF16),
            jax.ShapeDtypeStruct(full, BF16),
        ),
        in_specs=[pl.BlockSpec(memory_space=pltpu.SMEM)] + [anywhere] * 3 + [vmem] * 4 + [anywhere] * 2,
        out_specs=(anywhere,) * 4,
        scratch_shapes=[
            pltpu.VMEM(full, BF16), pltpu.VMEM(full, BF16), pltpu.VMEM(full, BF16), pltpu.VMEM((rows, model), BF16),
            pltpu.VMEM((rows, model), BF16), pltpu.VMEM(full, BF16), pltpu.VMEM(full, BF16), pltpu.VMEM(full, BF16),
            pltpu.VMEM((pairs, 256, model), BF16),
            pltpu.VMEM(full, F32), pltpu.VMEM(full, F32), pltpu.VMEM(full, F32), pltpu.VMEM(full, F32),
            pltpu.VMEM(full, BF16),
            pltpu.VMEM((rows, model), F32),
            pltpu.VMEM(full, F32), pltpu.VMEM(full, F32),
            pltpu.VMEM((3, 16, chan), BF16),
            pltpu.VMEM((3, 8, chan), F32), pltpu.VMEM((3, 8, chan), F32),
            pltpu.VMEM((2, chan), F32), pltpu.VMEM((REACH, 2, chan), F32),
            pltpu.VMEM((2, chan), F32), pltpu.VMEM((REACH, 2, chan), F32),
            dma((6,)), dma((2,)), dma((2, REACH)), dma((2, REACH)), dma,
            dma((count,)), dma((len(send_slots()) * Z_SIZE,)), dma((2, count)), dma((2,)), dma((4,)), dma((4,)),
        ],
        compiler_params=pltpu.CompilerParams(
            collective_id=0, has_side_effects=True, vmem_limit_bytes=60 * 1024 * 1024),
    )(doc_blocks, queries, key_inputs, values, short_taps, decay_rates, residues, skip_gain.reshape(1, chan),
      out_weight, cotangent)
    return pl.pallas_call(
        hand_on,
        out_shape=tuple(jax.ShapeDtypeStruct(o.shape, o.dtype) for o in outs),
        in_specs=[anywhere] * 4,
        out_specs=(anywhere,) * 4,
        scratch_shapes=[pltpu.VMEM(o.shape, o.dtype) for o in outs] + [dma((16,)), dma((16,))],
        compiler_params=pltpu.CompilerParams(vmem_limit_bytes=32 * 1024 * 1024),
    )(*outs)


def solution(mesh):
    rows = P(("groups", "seq"), None)
    return jax.shard_map(
        on_device,
        mesh=mesh,
        in_specs=(rows, rows, rows, P(), P(), P(), P(), P("seq", None), rows, P("groups")),
        out_specs=(rows, rows, rows, rows),
        check_vma=False,
    )
```
